32 devices in a mesh: section: 2 (over z_hi), dp: 8 (over y, x, core), tensor: 2 (over z_lo).
Axes of the slice: x: 2, y: 2, z: 4 (z_hi: 2, z_lo: 2; z = z_hi * 2 + z_lo), core: 2. Of those that a mesh axis runs over, the one named last changes fastest.
Arguments:
- hidden_in: bfloat16 [2, 1024, 8192], P('section', ('dp', 'tensor')), may hold values from -600 to 600
- norm_gain: bfloat16 [2, 8192], P('section'), may hold values from 0.5 to 1.5
- value_weight: bfloat16 [2, 8192, 512], P('section', 'dp', 'tensor'), may hold values from -0.0625 to 0.0625
- query_vectors: bfloat16 [2, 1024, 4096], P('section', 'dp', 'tensor'), may hold values from -9 to 9
- key_vectors: bfloat16 [2, 1024, 512], P('section', 'dp', 'tensor'), may hold values from -9 to 9
- grad_attn: bfloat16 [2, 1024, 4096], P('section', 'dp', 'tensor'), may hold values from -250 to 250
- positions: int32 [2, 1024], P('section', 'dp'), may hold values from 0 to 65535, as said below
Outputs:
- value_weight_grad: float32 [2, 8192, 512], P('section', 'dp', 'tensor')
- norm_gain_grad: float32 [2, 8192], P('section')
- to_previous: bfloat16 [2, 1024, 8192], P('section', ('dp', 'tensor'))
The draws below stay inside these ranges and needn't reach their ends.
Inputs may be any that keep to these rules, and one draw needn't show every extreme that they name: Within each micro-batch of 128 rows, positions rise by one from row to row except at one row between row 32 and row 95, where a new document starts at position 0.
All inputs are finite; a program needn't handle non-finite values.
Results may differ from the reference program's by a relative error of at most 0.014.
Values may be sent and summed in bfloat16 or wider, within the bound.
A program may use at most 64 MiB of HBM per device.

```python
import math
import jax
import jax.numpy as jnp
from jax import lax

D = 8192
HD = 128
KVH = 4
QPK = 8
QH = 32
KV = 512
TOK = 128
DOC = 65536
N_SECTION = 2
N_DP = 8
N_TENSOR = 2


def boundaries(key):
    return jax.random.randint(jax.random.fold_in(key, 101), (N_SECTION, N_DP), TOK // 4, 3 * TOK // 4).astype(jnp.int32)


def draw_positions(key, part):
    starts = boundaries(key)
    offsets = jax.random.randint(jax.random.fold_in(key, 102), (N_SECTION, N_DP), 0, DOC - TOK + 1).astype(jnp.int32)
    offsets = offsets.at[0, 0].set(DOC - starts[0, 0])
    places = jnp.arange(TOK, dtype=jnp.int32)
    first_piece = offsets[:, :, None] + places
    second_piece = places - starts[:, :, None]
    merged = jnp.where(places < starts[:, :, None], first_piece, second_piece)
    return merged.reshape(N_SECTION, N_DP * TOK).astype(jnp.int32)


def draw_query_vectors(key, part):
    shape_full = (N_SECTION, N_DP, TOK, KVH, QPK, HD)
    values = jnp.clip(jax.random.normal(jax.random.fold_in(key, 212), shape_full), -6.0, 6.0)
    return values.reshape(N_SECTION, N_DP * TOK, KVH * QPK * HD).astype(jnp.bfloat16)


def draw_key_vectors(key, part):
    shape_full = (N_SECTION, N_DP, TOK, KVH, HD)
    values = jnp.clip(jax.random.normal(jax.random.fold_in(key, 222), shape_full), -6.0, 6.0)
    return values.reshape(N_SECTION, N_DP * TOK, KVH * HD).astype(jnp.bfloat16)


def draw_grad_attn(key, part):
    shape_full = (N_SECTION, N_DP * TOK, QH * HD)
    rising = 3.0 ** (jnp.arange(N_DP * TOK, dtype=jnp.float32) / (N_DP * TOK))
    values = jnp.clip(jax.random.normal(jax.random.fold_in(key, 303), shape_full), -6.0, 6.0)
    values = values * rising[:, None] * 4.0
    return values.astype(jnp.bfloat16)


def draw_hidden_in(key, part):
    shape_full = (N_SECTION, N_DP * TOK, D)
    values = jnp.clip(jax.random.normal(jax.random.fold_in(key, 404), shape_full), -6.0, 6.0)
    return values.astype(jnp.bfloat16)


def block_scale(rng, extent, shards, least, high):
    def one(axis_at, parts):
        draws = jax.random.uniform(jax.random.fold_in(jax.random.fold_in(rng, 6), axis_at), (parts,), jnp.float32, least / len(shards), high / len(shards))
        return jnp.repeat(jnp.exp(draws), extent[axis_at] // parts).reshape((-1,) + (1,) * (len(extent) - axis_at - 1))

    factor_of = one(*shards[0])
    for cut in shards[1:]:
        factor_of = factor_of * one(*cut)
    return factor_of


def scatter_about(key, dims, deviation, reach, shards=(), kind=jnp.bfloat16):
    array = deviation * jax.random.normal(key, dims, jnp.float32)
    if shards:
        array = array * block_scale(key, dims, shards, -0.22, 0.18)
    return jnp.clip(array, -reach, reach).astype(kind)


def setup_inputs(seed: int = 0) -> dict:
    streams_of = jax.random.split(jax.random.key(seed), 8)
    hidden_in = draw_hidden_in(jax.random.fold_in(streams_of[7], 71), 0)
    norm_gain = jnp.clip(1.0 + 0.1 * jax.random.normal(streams_of[1], (N_SECTION, D), jnp.float32), 0.5, 1.5).astype(jnp.bfloat16)
    value_weight = scatter_about(streams_of[2], (N_SECTION, D, KV), D ** -0.5, 0.0625, ((0, 2), (1, 8), (2, 2)))
    query_vectors = draw_query_vectors(jax.random.fold_in(streams_of[7], 71), 0)
    key_vectors = draw_key_vectors(jax.random.fold_in(streams_of[7], 71), 0)
    grad_attn = draw_grad_attn(jax.random.fold_in(streams_of[7], 71), 0)
    positions = draw_positions(jax.random.fold_in(streams_of[7], 71), 0)
    return dict(hidden_in=hidden_in, norm_gain=norm_gain, value_weight=value_weight, query_vectors=query_vectors, key_vectors=key_vectors, grad_attn=grad_attn, positions=positions)


def attend(operands):
    query_rows, key_rows, grad_rows, position_rows = operands
    length = query_rows.shape[0]
    groups = key_rows.shape[1] // HD
    query_heads = query_rows.astype(jnp.float32).reshape(length, groups, QPK, HD)
    key_heads = key_rows.astype(jnp.float32).reshape(length, groups, HD)
    grad_heads = grad_rows.astype(jnp.float32).reshape(length, groups, QPK, HD)
    scores = jnp.einsum('igpd,jgd->gpij', query_heads, key_heads) / math.sqrt(HD)
    places = jnp.arange(length, dtype=jnp.int32)
    visible = (places[:, None] >= places[None, :]) & (position_rows[:, None] - position_rows[None, :] == places[:, None] - places[None, :])
    masked = jnp.where(visible, scores, jnp.float32(-1e+30))
    largest = lax.optimization_barrier(jnp.max(masked, axis=-1, keepdims=True))
    powers = jnp.where(visible, jnp.exp(masked - largest), jnp.float32(0.0))
    probabilities = powers / lax.optimization_barrier(jnp.sum(powers, axis=-1, keepdims=True))
    weights = lax.optimization_barrier(probabilities.astype(jnp.bfloat16)).astype(jnp.float32)
    value_grad = jnp.einsum('gpij,igpd->jgd', weights, grad_heads)
    return value_grad.reshape(length, groups * HD).astype(jnp.bfloat16)

def one_section(operands):
    hidden_in, norm_gain, value_weight, query_vectors, key_vectors, grad_attn, positions = operands
    rows_float = hidden_in.astype(jnp.float32)
    root_mean = jnp.sqrt(lax.optimization_barrier(jnp.mean(rows_float * rows_float, axis=1, keepdims=True)) + 1e-05)
    normed = rows_float / root_mean
    gain_float = norm_gain.astype(jnp.float32)
    layer_input = (normed * gain_float).astype(jnp.bfloat16)

    def batched(stacked):
        return stacked.reshape((N_DP, TOK) + stacked.shape[1:])
    value_grad = lax.map(attend, (batched(query_vectors), batched(key_vectors), batched(grad_attn), batched(positions)))

    def add_term(running, pieces):
        inputs, gradients = pieces
        partial_term = jnp.dot(inputs.T, gradients, preferred_element_type=jnp.float32).astype(jnp.bfloat16)
        return (running + lax.optimization_barrier(partial_term).astype(jnp.float32), None)
    weight_grad, _ = lax.scan(add_term, jnp.zeros((D, KV), jnp.float32), (batched(layer_input), value_grad))
    value_flat = value_grad.reshape(N_DP * TOK, KV)
    group_width = KV // N_TENSOR
    grad_input = jnp.zeros((N_DP * TOK, D), jnp.float32)
    for column_group in range(N_TENSOR):
        first_column = column_group * group_width
        partial_term = jnp.dot(value_flat[:, first_column:first_column + group_width], value_weight[:, first_column:first_column + group_width].T, preferred_element_type=jnp.float32).astype(jnp.bfloat16)
        grad_input = grad_input + lax.optimization_barrier(partial_term).astype(jnp.float32)
    gain_grad = lax.optimization_barrier(jnp.sum(grad_input * normed, axis=0))
    grad_normed = grad_input * gain_float
    inner_mean = lax.optimization_barrier(jnp.mean(grad_normed * normed, axis=1, keepdims=True))
    grad_hidden = ((grad_normed - normed * inner_mean) / root_mean).astype(jnp.bfloat16)
    return (weight_grad, gain_grad, grad_hidden)

def reference(hidden_in, norm_gain, value_weight, query_vectors, key_vectors, grad_attn, positions):
    weight_grad, gain_grad, grad_hidden = lax.map(one_section, (hidden_in, norm_gain, value_weight, query_vectors, key_vectors, grad_attn, positions))
    to_previous = jnp.concatenate([grad_hidden[1:], jnp.zeros_like(grad_hidden[:1])], axis=0)
    return (weight_grad, gain_grad, to_previous)
```

```python
import functools
import math

import jax
import jax.numpy as jnp
from jax import lax
from jax.experimental import pallas as pl
from jax.experimental.pallas import tpu as pltpu
from jax.sharding import PartitionSpec as P

HD = 128
QPK = 8
LANES = 128
MESH = pl.DeviceIdType.MESH


def dot(left, right, dims):
    return lax.dot_general(left, right, (dims, ((), ())), preferred_element_type=jnp.float32)


def kernel(
    sizes, hidden, gain, weight, query, key, grad, positions,
    weight_out, gain_out, previous,
    hid, values, value_own, weights, grad_in, inverse, stats, finished, term_send, term_recv,
    gain_parts,
    hid_send, hid_recv, wt_send, wt_recv, val_send, val_recv, stat_send, stat_recv,
    out_send, out_recv, term_ssem, term_rsem, gain_send, gain_recv, local_sem,
):
    ns, nd, nt = sizes
    section, me, col = (lax.axis_index(axis) for axis in ("section", "dp", "tensor"))
    rows = hidden.shape[1]
    features = weight.shape[1]
    width = weight.shape[2]
    tokens = rows * nd
    model = features * nd
    blocks = tokens // LANES
    per_block = LANES // rows
    chunk = min(256, features)
    chunks = features // chunk

    def dp_peer(step):
        return lax.rem(me + step, nd)

    def col_peer(step):
        return lax.rem(col + step, nt)

    barrier = pltpu.get_barrier_semaphore()

    def greet(step, carry):
        target = lax.rem(me * nt + col + step, nd * nt)
        pl.semaphore_signal(
            barrier, inc=1, device_id={"dp": target // nt, "tensor": lax.rem(target, nt)},
            device_id_type=MESH,
        )
        return carry

    lax.fori_loop(1, nd * nt, greet, 0)

    @pl.when(section < ns - 1)
    def _():
        def greet_next(step, carry):
            pl.semaphore_signal(
                barrier, inc=1, device_id={"section": section + 1, "dp": dp_peer(step)},
                device_id_type=MESH,
            )
            return carry

        lax.fori_loop(0, nd, greet_next, 0)

    pl.semaphore_wait(barrier, nd * nt - 1 + nd * jnp.minimum(section, 1))

    def row_slice(index):
        return pl.ds(pl.multiple_of(index * rows, rows), rows)

    def feature_slice(index):
        return pl.ds(pl.multiple_of(index * features, features), features)

    def hid_copy(target, source):
        return pltpu.make_async_remote_copy(
            src_ref=hidden.at[0, :, feature_slice(target)], dst_ref=hid.at[row_slice(source), :],
            send_sem=hid_send.at[target], recv_sem=hid_recv.at[source],
            device_id={"dp": target}, device_id_type=MESH,
        )

    def weight_copy(target, source):
        return pltpu.make_async_remote_copy(
            src_ref=weight.at[0], dst_ref=weights.at[source],
            send_sem=wt_send.at[target], recv_sem=wt_recv.at[source],
            device_id={"tensor": target}, device_id_type=MESH,
        )

    def value_copy(target_dp, target_col, source_dp, source_col):
        return pltpu.make_async_remote_copy(
            src_ref=value_own.at[target_col],
            dst_ref=values.at[source_col, row_slice(source_dp), :],
            send_sem=val_send.at[target_col, target_dp], recv_sem=val_recv.at[source_col, source_dp],
            device_id={"dp": target_dp, "tensor": target_col}, device_id_type=MESH,
        )

    def stat_copy(target, source):
        return pltpu.make_async_remote_copy(
            src_ref=stats.at[me], dst_ref=stats.at[source],
            send_sem=stat_send.at[target], recv_sem=stat_recv.at[source],
            device_id={"dp": target}, device_id_type=MESH,
        )

    def out_copy(target, source):
        return pltpu.make_async_remote_copy(
            src_ref=finished.at[row_slice(target), :],
            dst_ref=previous.at[:, feature_slice(source)],
            send_sem=out_send.at[target], recv_sem=out_recv.at[source],
            device_id={"section": jnp.maximum(section - 1, 0), "dp": target}, device_id_type=MESH,
        )

    def term_copy(target, source):
        return pltpu.make_async_remote_copy(
            src_ref=term_send.at[target], dst_ref=term_recv.at[source],
            send_sem=term_ssem.at[target], recv_sem=term_rsem.at[source],
            device_id={"tensor": target}, device_id_type=MESH,
        )

    def gain_copy(target_dp, target_col, source_dp, source_col):
        return pltpu.make_async_remote_copy(
            src_ref=gain_parts.at[col, me], dst_ref=gain_parts.at[source_col, source_dp],
            send_sem=gain_send.at[target_col, target_dp],
            recv_sem=gain_recv.at[source_col, source_dp],
            device_id={"dp": target_dp, "tensor": target_col}, device_id_type=MESH,
        )

    def loop(first, last, body):
        def run(step, carry):
            body(step)
            return carry

        lax.fori_loop(first, last, run, 0)

    def over_section(body):
        def run(step):
            target = lax.rem(me * nt + col + step, nd * nt)
            body(target // nt, lax.rem(target, nt))

        loop(1, nd * nt, run)

    loop(1, nd, lambda step: hid_copy(dp_peer(step), me).start())
    loop(1, nt, lambda step: weight_copy(col_peer(step), col).start())
    own_hid = pltpu.make_async_copy(
        hidden.at[0, :, feature_slice(me)], hid.at[row_slice(me), :], local_sem.at[0]
    )
    own_hid.start()
    own_weight = pltpu.make_async_copy(weight.at[0], weights.at[col], local_sem.at[1])
    own_weight.start()

    @pl.when(section == ns - 1)
    def _():
        previous[...] = jnp.zeros_like(previous)

    length = query.shape[1]
    down = lax.broadcasted_iota(jnp.int32, (length, length), 0)
    across = lax.broadcasted_iota(jnp.int32, (length, length), 1)
    base_across = jnp.broadcast_to(positions[...], (length, length)) - across
    visible = (down <= across) & (base_across == base_across.T)
    for group in range(width // HD):
        key_rows = key[0, :, group * HD : (group + 1) * HD]
        total = jnp.zeros((length, HD), jnp.float32)
        for head in range(QPK):
            first = (group * QPK + head) * HD
            scores = dot(key_rows, query[0, :, first : first + HD], ((1,), (1,)))
            masked = jnp.where(visible, scores / math.sqrt(HD), jnp.float32(-1e30))
            largest = jnp.max(masked, axis=0, keepdims=True)
            powers = jnp.where(visible, jnp.exp(masked - largest), jnp.float32(0.0))
            probabilities = powers / jnp.sum(powers, axis=0, keepdims=True)
            total = total + dot(
                probabilities.astype(jnp.bfloat16), grad[0, :, first : first + HD], ((1,), (0,))
            )
        rounded = total.astype(jnp.bfloat16)
        for part in range(nt):
            value_own[part, :, group * HD : (group + 1) * HD] = rounded[
                part * rows : (part + 1) * rows
            ]

    over_section(lambda dp, tensor: value_copy(dp, tensor, me, col).start())
    values[col, row_slice(me), :] = value_own[col]

    own_hid.wait()
    own_weight.wait()
    loop(1, nt, lambda step: weight_copy(col_peer(step), col_peer(step)).wait_recv())
    loop(1, nd, lambda step: hid_copy(dp_peer(step), dp_peer(step)).wait_recv())
    over_section(lambda dp, tensor: value_copy(dp, tensor, dp, tensor).wait_recv())

    def gain_row(start, size):
        place = pl.multiple_of(me * features + start, LANES)
        return gain[:, pl.ds(place, size)].astype(jnp.float32)

    def fold(array):
        out = array[:, :LANES]
        for at in range(LANES, array.shape[1], LANES):
            out = out + array[:, at : at + LANES]
        return out

    products = [jnp.zeros((LANES, LANES), jnp.float32) for _ in range(blocks)]
    squares = [jnp.zeros((LANES, LANES), jnp.float32) for _ in range(blocks)]
    for piece in range(chunks):
        at = piece * chunk
        terms = jnp.zeros((tokens, chunk), jnp.float32)
        for part in range(nt):
            terms = terms + dot(values[part], weights[part, at : at + chunk, :], ((1,), (1,)))
        grad_in[:, at : at + chunk] = terms
        scaled = gain_row(at, chunk)
        for block in range(blocks):
            span = slice(block * LANES, (block + 1) * LANES)
            inputs = hid[span, at : at + chunk].astype(jnp.float32)
            products[block] = products[block] + fold(terms[span] * scaled * inputs)
            squares[block] = squares[block] + fold(inputs * inputs)
    for block in range(blocks):
        stats[me, block : block + 1, :] = jnp.sum(products[block].T, axis=0, keepdims=True)
        stats[me, blocks + block : blocks + block + 1, :] = jnp.sum(
            squares[block].T, axis=0, keepdims=True
        )

    loop(1, nd, lambda step: stat_copy(dp_peer(step), me).start())
    loop(1, nd, lambda step: stat_copy(dp_peer(step), dp_peer(step)).wait_recv())

    totals = stats[0]
    for index in range(1, nd):
        totals = totals + stats[index]
    mean_square = totals[blocks:] / model + 1e-05
    root = jnp.sqrt(mean_square)
    stretch = 1.0 / root
    inner = totals[:blocks] / model / mean_square

    def column(rows_of, block):
        return jnp.broadcast_to(rows_of[block : block + 1], (LANES, LANES)).T

    for block in range(blocks):
        span = slice(block * LANES, (block + 1) * LANES)
        inverse[0, span, :] = column(stretch, block)
        inverse[1, span, :] = column(inner, block)

    def finish(step):
        block = lax.rem(me // per_block + step, blocks)
        span = pl.ds(pl.multiple_of(block * LANES, LANES), LANES)
        scale = inverse[0, span, :]
        mean = inverse[1, span, :]
        for at in range(0, features, LANES):
            lanes = slice(at, at + LANES)
            normal = grad_in[span, lanes] * gain_row(at, LANES)
            inputs = hid[span, lanes].astype(jnp.float32)
            finished[span, lanes] = ((normal - inputs * mean) * scale).astype(jnp.bfloat16)

        @pl.when(section > 0)
        def _():
            for part in range(per_block):
                out_copy(block * per_block + part, me).start()

    loop(0, blocks, finish)

    for piece in range(chunks):
        at = piece * chunk
        scaled = gain_row(at, chunk)
        parts = []
        sums = jnp.zeros((1, chunk), jnp.float32)
        for block in range(blocks):
            span = slice(block * LANES, (block + 1) * LANES)
            scale = jnp.concatenate([inverse[0, span, :]] * (chunk // LANES), axis=1)
            normed = hid[span, at : at + chunk].astype(jnp.float32) * scale
            parts.append((normed * scaled).astype(jnp.bfloat16))
            sums = sums + jnp.sum(
                grad_in[span, at : at + chunk] * normed, axis=0, keepdims=True
            )
        gain_parts[col, me, :, at : at + chunk] = sums
        inputs = jnp.concatenate(parts, axis=0)
        weight_out[0, at : at + chunk, :] = dot(inputs, values[col], ((0,), (0,)))
        for step in range(1, nt):
            target = col_peer(step)
            term_send[target, at : at + chunk, :] = dot(
                inputs, values[target], ((0,), (0,))
            ).astype(jnp.bfloat16)

    loop(1, nt, lambda step: term_copy(col_peer(step), col).start())
    over_section(lambda dp, tensor: gain_copy(dp, tensor, me, col).start())

    for step in range(1, nt):
        term_copy(col_peer(step), col_peer(step)).wait_recv()
        weight_out[0] += term_recv[col_peer(step)].astype(jnp.float32)
    over_section(lambda dp, tensor: gain_copy(dp, tensor, dp, tensor).wait_recv())
    for index in range(nd):
        total = gain_parts[0, index]
        for part in range(1, nt):
            total = total + gain_parts[part, index]
        gain_out[:, index * features : (index + 1) * features] = total

    loop(1, nd, lambda step: hid_copy(dp_peer(step), me).wait_send())
    loop(1, nt, lambda step: weight_copy(col_peer(step), col).wait_send())
    over_section(lambda dp, tensor: value_copy(dp, tensor, me, col).wait_send())
    loop(1, nd, lambda step: stat_copy(dp_peer(step), me).wait_send())
    loop(1, nt, lambda step: term_copy(col_peer(step), col).wait_send())
    over_section(lambda dp, tensor: gain_copy(dp, tensor, me, col).wait_send())

    @pl.when(section < ns - 1)
    def _():
        loop(0, nd, lambda step: out_copy(dp_peer(step), dp_peer(step)).wait_recv())

    @pl.when(section > 0)
    def _():
        loop(0, nd, lambda step: out_copy(dp_peer(step), me).wait_send())


def shards(sizes, hidden_in, norm_gain, value_weight, query, key, grad, positions):
    ns, nd, nt = sizes
    rows, model = hidden_in.shape[1:]
    features, width = value_weight.shape[1:]
    tokens = rows * nd
    vmem = pl.BlockSpec(memory_space=pltpu.VMEM)
    dma = pltpu.SemaphoreType.DMA
    return pl.pallas_call(
        functools.partial(kernel, sizes),
        out_shape=(
            jax.ShapeDtypeStruct(value_weight.shape, jnp.float32),
            jax.ShapeDtypeStruct(norm_gain.shape, jnp.float32),
            jax.ShapeDtypeStruct((rows, model), jnp.bfloat16),
        ),
        in_specs=[vmem] * 7,
        out_specs=(vmem, vmem, vmem),
        scratch_shapes=[
            pltpu.VMEM((tokens, features), jnp.bfloat16),
            pltpu.VMEM((nt, tokens, width), jnp.bfloat16),
            pltpu.VMEM((nt, rows, width), jnp.bfloat16),
            pltpu.VMEM((nt, features, width), jnp.bfloat16),
            pltpu.VMEM((tokens, features), jnp.float32),
            pltpu.VMEM((2, tokens, LANES), jnp.float32),
            pltpu.VMEM((nd, 2 * tokens // LANES, LANES), jnp.float32),
            pltpu.VMEM((tokens, features), jnp.bfloat16),
            pltpu.VMEM((nt, features, width), jnp.bfloat16),
            pltpu.VMEM((nt, features, width), jnp.bfloat16),
            pltpu.VMEM((nt, nd, 1, features), jnp.float32),
            dma((nd,)), dma((nd,)), dma((nt,)), dma((nt,)),
            dma((nt, nd)), dma((nt, nd)), dma((nd,)), dma((nd,)),
            dma((nd,)), dma((nd,)), dma((nt,)), dma((nt,)),
            dma((nt, nd)), dma((nt, nd)), dma((2,)),
        ],
        compiler_params=pltpu.CompilerParams(
            collective_id=0, has_side_effects=True, vmem_limit_bytes=48 * 1024 * 1024
        ),
        name="value_path_backward",
    )(hidden_in, norm_gain, value_weight, query, key, grad, positions)


def solution(mesh):
    sizes = tuple(mesh.shape[axis] for axis in ("section", "dp", "tensor"))

    def local(hidden_in, norm_gain, value_weight, query, key, grad, positions):
        weight_grad, gain_grad, previous = shards(
            sizes, hidden_in, norm_gain, value_weight, query, key, grad, positions
        )
        return (weight_grad, gain_grad, previous[None])

    return jax.shard_map(
        local,
        mesh=mesh,
        in_specs=(
            P("section", ("dp", "tensor"), None),
            P("section", None),
            P("section", "dp", "tensor"),
            P("section", "dp", "tensor"),
            P("section", "dp", "tensor"),
            P("section", "dp", "tensor"),
            P("section", "dp"),
        ),
        out_specs=(
            P("section", "dp", "tensor"),
            P("section", None),
            P("section", ("dp", "tensor"), None),
        ),
        check_vma=False,
    )
```

```python
import functools
import math

import jax
import jax.numpy as jnp
from jax import lax
from jax.experimental import pallas as pl
from jax.experimental.pallas import tpu as pltpu
from jax.sharding import PartitionSpec as P

HD = 128
QPK = 8
PARTS = 2
LANES = 128
MESH = pl.DeviceIdType.MESH


def dot(left, right, dims):
    return lax.dot_general(left, right, (dims, ((), ())), preferred_element_type=jnp.float32)


def kernel(
    sizes, hidden, gain, weight, query_hbm, key_hbm, grad_hbm, positions_hbm,
    weight_out, gain_out, previous,
    query, key, grad, positions, hid, values, value_own, weights, grad_in, inverse, stats, finished, term_send, term_recv,
    gain_parts,
    hid_send, hid_recv, wt_send, wt_recv, val_send, val_recv, stat_send, stat_recv,
    out_send, out_recv, term_ssem, term_rsem, gain_send, gain_recv, local_sem,
):
    ns, nd, nt = sizes
    section, me, col = (lax.axis_index(axis) for axis in ("section", "dp", "tensor"))
    rows = hidden.shape[1]
    features = weight.shape[1]
    width = weight.shape[2]
    sub = rows // PARTS
    tokens = sub * nd
    model = features * nd
    blocks = tokens // LANES
    chunk = min(256, features)
    chunks = features // chunk

    def dp_peer(step):
        return lax.rem(me + step, nd)

    def col_peer(step):
        return lax.rem(col + step, nt)

    fetches = [
        pltpu.make_async_copy(source, target, local_sem.at[1 + index])
        for index, (source, target) in enumerate(
            [
                (positions_hbm, positions), (key_hbm.at[0], key),
                (query_hbm.at[0], query), (grad_hbm.at[0], grad),
            ]
        )
    ]
    for fetch in fetches:
        fetch.start()

    barrier = pltpu.get_barrier_semaphore()

    def greet(step, carry):
        target = lax.rem(me * nt + col + step, nd * nt)
        pl.semaphore_signal(
            barrier, inc=1, device_id={"dp": target // nt, "tensor": lax.rem(target, nt)},
            device_id_type=MESH,
        )
        return carry

    lax.fori_loop(1, nd * nt, greet, 0)

    @pl.when(section < ns - 1)
    def _():
        def greet_next(step, carry):
            pl.semaphore_signal(
                barrier, inc=1, device_id={"section": section + 1, "dp": dp_peer(step)},
                device_id_type=MESH,
            )
            return carry

        lax.fori_loop(0, nd, greet_next, 0)

    pl.semaphore_wait(barrier, nd * nt - 1 + nd * jnp.minimum(section, 1))

    def row_slice(index):
        return pl.ds(pl.multiple_of(index * sub, sub), sub)

    def feature_slice(index):
        return pl.ds(pl.multiple_of(index * features, features), features)

    def hid_copy(part, target, source):
        return pltpu.make_async_remote_copy(
            src_ref=hidden.at[0, part * sub : (part + 1) * sub, feature_slice(target)],
            dst_ref=hid.at[part, row_slice(source), :],
            send_sem=hid_send.at[part, target], recv_sem=hid_recv.at[part, source],
            device_id={"dp": target}, device_id_type=MESH,
        )

    def weight_copy(target, source):
        return pltpu.make_async_remote_copy(
            src_ref=weight.at[0], dst_ref=weights.at[source],
            send_sem=wt_send.at[target], recv_sem=wt_recv.at[source],
            device_id={"tensor": target}, device_id_type=MESH,
        )

    def value_copy(part, target_dp, target_col, source_dp, source_col):
        return pltpu.make_async_remote_copy(
            src_ref=value_own.at[target_col, part],
            dst_ref=values.at[part, source_col, row_slice(source_dp), :],
            send_sem=val_send.at[part, target_col, target_dp],
            recv_sem=val_recv.at[part, source_col, source_dp],
            device_id={"dp": target_dp, "tensor": target_col}, device_id_type=MESH,
        )

    def stat_copy(part, target, source):
        return pltpu.make_async_remote_copy(
            src_ref=stats.at[part, me], dst_ref=stats.at[part, source],
            send_sem=stat_send.at[part, target], recv_sem=stat_recv.at[part, source],
            device_id={"dp": target}, device_id_type=MESH,
        )

    def out_copy(part, target, source):
        return pltpu.make_async_remote_copy(
            src_ref=finished.at[part, row_slice(target), :],
            dst_ref=previous.at[part * sub : (part + 1) * sub, feature_slice(source)],
            send_sem=out_send.at[part, target], recv_sem=out_recv.at[part, source],
            device_id={"section": jnp.maximum(section - 1, 0), "dp": target}, device_id_type=MESH,
        )

    def term_copy(target, source):
        return pltpu.make_async_remote_copy(
            src_ref=term_send.at[target], dst_ref=term_recv.at[source],
            send_sem=term_ssem.at[target], recv_sem=term_rsem.at[source],
            device_id={"tensor": target}, device_id_type=MESH,
        )

    def gain_copy(target_dp, target_col, source_dp, source_col):
        return pltpu.make_async_remote_copy(
            src_ref=gain_parts.at[col, me], dst_ref=gain_parts.at[source_col, source_dp],
            send_sem=gain_send.at[target_col, target_dp],
            recv_sem=gain_recv.at[source_col, source_dp],
            device_id={"dp": target_dp, "tensor": target_col}, device_id_type=MESH,
        )

    def loop(first, last, body):
        def run(step, carry):
            body(step)
            return carry

        lax.fori_loop(first, last, run, 0)

    def over_section(body):
        def run(step):
            target = lax.rem(me * nt + col + step, nd * nt)
            body(target // nt, lax.rem(target, nt))

        loop(1, nd * nt, run)

    loop(1, nd, lambda step: hid_copy(0, dp_peer(step), me).start())
    loop(1, nt, lambda step: weight_copy(col_peer(step), col).start())
    own_hid = [
        pltpu.make_async_copy(
            hidden.at[0, part * sub : (part + 1) * sub, feature_slice(me)],
            hid.at[part, row_slice(me), :], hid_recv.at[part, me],
        )
        for part in range(PARTS)
    ]
    for copy in own_hid:
        copy.start()
    own_weight = pltpu.make_async_copy(weight.at[0], weights.at[col], local_sem.at[0])
    own_weight.start()

    @pl.when(section == ns - 1)
    def _():
        previous[...] = jnp.zeros_like(previous)

    for fetch in fetches:
        fetch.wait()
    length = query.shape[0]
    down = lax.broadcasted_iota(jnp.int32, (length, length), 0)
    across = lax.broadcasted_iota(jnp.int32, (length, length), 1)
    base_across = jnp.broadcast_to(positions[...], (length, length)) - across
    visible = (down <= across) & (base_across == base_across.T)
    for group in range(width // HD):
        key_rows = key[:, group * HD : (group + 1) * HD]
        total = jnp.zeros((length, HD), jnp.float32)
        for head in range(QPK):
            first = (group * QPK + head) * HD
            scores = dot(key_rows, query[:, first : first + HD], ((1,), (1,)))
            masked = jnp.where(visible, scores / math.sqrt(HD), jnp.float32(-1e30))
            largest = jnp.max(masked, axis=0, keepdims=True)
            powers = jnp.where(visible, jnp.exp(masked - largest), jnp.float32(0.0))
            probabilities = powers / jnp.sum(powers, axis=0, keepdims=True)
            total = total + dot(
                probabilities.astype(jnp.bfloat16), grad[:, first : first + HD], ((1,), (0,))
            )
        rounded = total.astype(jnp.bfloat16)
        for tensor in range(nt):
            for part in range(PARTS):
                first = tensor * rows + part * sub
                value_own[tensor, part, :, group * HD : (group + 1) * HD] = rounded[
                    first : first + sub
                ]

    def send_values(part):
        over_section(lambda dp, tensor: value_copy(part, dp, tensor, me, col).start())
        values[part, col, row_slice(me), :] = value_own[col, part]

    def send_later():
        for part in range(1, PARTS):
            loop(1, nd, lambda step: hid_copy(part, dp_peer(step), me).start())
            send_values(part)

    send_values(0)
    send_later()
    own_weight.wait()
    loop(1, nt, lambda step: weight_copy(col_peer(step), col_peer(step)).wait_recv())

    def gain_row(start, size):
        place = pl.multiple_of(me * features + start, LANES)
        return gain[:, pl.ds(place, size)].astype(jnp.float32)

    def fold(array):
        out = array[:, :LANES]
        for at in range(LANES, array.shape[1], LANES):
            out = out + array[:, at : at + LANES]
        return out

    def column(rows_of, block):
        return jnp.broadcast_to(rows_of[block : block + 1], (LANES, LANES)).T

    def multiply(part):
        own_hid[part].wait()
        loop(1, nd, lambda step: hid_copy(part, dp_peer(step), dp_peer(step)).wait_recv())
        over_section(lambda dp, tensor: value_copy(part, dp, tensor, dp, tensor).wait_recv())
        products = [jnp.zeros((LANES, LANES), jnp.float32) for _ in range(blocks)]
        squares = [jnp.zeros((LANES, LANES), jnp.float32) for _ in range(blocks)]
        for piece in range(chunks):
            at = piece * chunk
            terms = jnp.zeros((tokens, chunk), jnp.float32)
            for tensor in range(nt):
                terms = terms + dot(
                    values[part, tensor], weights[tensor, at : at + chunk, :], ((1,), (1,))
                )
            grad_in[part, :, at : at + chunk] = terms
            scaled = gain_row(at, chunk)
            for block in range(blocks):
                span = slice(block * LANES, (block + 1) * LANES)
                inputs = hid[part, span, at : at + chunk].astype(jnp.float32)
                products[block] = products[block] + fold(terms[span] * scaled * inputs)
                squares[block] = squares[block] + fold(inputs * inputs)
        for block in range(blocks):
            stats[part, me, block : block + 1, :] = jnp.sum(
                products[block].T, axis=0, keepdims=True
            )
            stats[part, me, blocks + block : blocks + block + 1, :] = jnp.sum(
                squares[block].T, axis=0, keepdims=True
            )

        loop(1, nd, lambda step: stat_copy(part, dp_peer(step), me).start())

    def finish(part):
        loop(1, nd, lambda step: stat_copy(part, dp_peer(step), dp_peer(step)).wait_recv())

        totals = stats[part, 0]
        for index in range(1, nd):
            totals = totals + stats[part, index]
        mean_square = totals[blocks:] / model + 1e-05
        stretch = 1.0 / jnp.sqrt(mean_square)
        inner = totals[:blocks] / model / mean_square

        for block in range(blocks):
            span = slice(block * LANES, (block + 1) * LANES)
            scale = column(stretch, block)
            mean = column(inner, block)
            inverse[part, span, :] = scale
            for at in range(0, features, LANES):
                lanes = slice(at, at + LANES)
                normal = grad_in[part, span, lanes] * gain_row(at, LANES)
                inputs = hid[part, span, lanes].astype(jnp.float32)
                finished[part, span, lanes] = ((normal - inputs * mean) * scale).astype(
                    jnp.bfloat16
                )

    def send_out(part, first, last):
        @pl.when(section > 0)
        def _():
            loop(first, last, lambda step: out_copy(part, dp_peer(step), me).start())

    multiply(0)
    finish(0)
    ahead = max(1, nd * 3 // 8)
    send_out(0, 0, ahead)
    multiply(1)
    send_out(0, ahead, nd)
    finish(1)
    send_out(1, 0, nd)

    for piece in range(chunks):
        at = piece * chunk
        scaled = gain_row(at, chunk)
        inputs = []
        sums = jnp.zeros((1, chunk), jnp.float32)
        for part in range(PARTS):
            pieces = []
            for block in range(blocks):
                span = slice(block * LANES, (block + 1) * LANES)
                scale = jnp.concatenate([inverse[part, span, :]] * (chunk // LANES), axis=1)
                normed = hid[part, span, at : at + chunk].astype(jnp.float32) * scale
                pieces.append((normed * scaled).astype(jnp.bfloat16))
                sums = sums + jnp.sum(
                    grad_in[part, span, at : at + chunk] * normed, axis=0, keepdims=True
                )
            inputs.append(jnp.concatenate(pieces, axis=0))
        gain_parts[col, me, :, at : at + chunk] = sums
        for step in range(nt):
            target = col_peer(step)
            terms = dot(inputs[0], values[0, target], ((0,), (0,)))
            for part in range(1, PARTS):
                terms = terms + dot(inputs[part], values[part, target], ((0,), (0,)))
            if step == 0:
                weight_out[0, at : at + chunk, :] = terms
            else:
                term_send[target, at : at + chunk, :] = terms.astype(jnp.bfloat16)

    loop(1, nt, lambda step: term_copy(col_peer(step), col).start())
    over_section(lambda dp, tensor: gain_copy(dp, tensor, me, col).start())

    for step in range(1, nt):
        term_copy(col_peer(step), col_peer(step)).wait_recv()
        weight_out[0] += term_recv[col_peer(step)].astype(jnp.float32)
    over_section(lambda dp, tensor: gain_copy(dp, tensor, dp, tensor).wait_recv())
    for index in range(nd):
        total = gain_parts[0, index]
        for part in range(1, nt):
            total = total + gain_parts[part, index]
        gain_out[:, index * features : (index + 1) * features] = total

    for part in range(PARTS):
        loop(1, nd, lambda step: hid_copy(part, dp_peer(step), me).wait_send())
        over_section(lambda dp, tensor: value_copy(part, dp, tensor, me, col).wait_send())
        loop(1, nd, lambda step: stat_copy(part, dp_peer(step), me).wait_send())
    loop(1, nt, lambda step: weight_copy(col_peer(step), col).wait_send())
    loop(1, nt, lambda step: term_copy(col_peer(step), col).wait_send())
    over_section(lambda dp, tensor: gain_copy(dp, tensor, me, col).wait_send())

    @pl.when(section < ns - 1)
    def _():
        for part in range(PARTS):
            loop(0, nd, lambda step: out_copy(part, dp_peer(step), dp_peer(step)).wait_recv())

    @pl.when(section > 0)
    def _():
        for part in range(PARTS):
            loop(0, nd, lambda step: out_copy(part, dp_peer(step), me).wait_send())


def shards(sizes, hidden_in, norm_gain, value_weight, query, key, grad, positions):
    ns, nd, nt = sizes
    rows, model = hidden_in.shape[1:]
    features, width = value_weight.shape[1:]
    sub = rows // PARTS
    tokens = sub * nd
    vmem = pl.BlockSpec(memory_space=pltpu.VMEM)
    hbm = pl.BlockSpec(memory_space=pltpu.HBM)
    dma = pltpu.SemaphoreType.DMA
    return pl.pallas_call(
        functools.partial(kernel, sizes),
        out_shape=(
            jax.ShapeDtypeStruct(value_weight.shape, jnp.float32),
            jax.ShapeDtypeStruct(norm_gain.shape, jnp.float32),
            jax.ShapeDtypeStruct((rows, model), jnp.bfloat16),
        ),
        in_specs=[hbm, vmem, hbm, hbm, hbm, hbm, hbm],
        out_specs=(vmem, vmem, vmem),
        scratch_shapes=[
            pltpu.VMEM(query.shape[1:], jnp.bfloat16),
            pltpu.VMEM(key.shape[1:], jnp.bfloat16),
            pltpu.VMEM(grad.shape[1:], jnp.bfloat16),
            pltpu.VMEM(positions.shape, jnp.int32),
            pltpu.VMEM((PARTS, tokens, features), jnp.bfloat16),
            pltpu.VMEM((PARTS, nt, tokens, width), jnp.bfloat16),
            pltpu.VMEM((nt, PARTS, sub, width), jnp.bfloat16),
            pltpu.VMEM((nt, features, width), jnp.bfloat16),
            pltpu.VMEM((PARTS, tokens, features), jnp.float32),
            pltpu.VMEM((PARTS, tokens, LANES), jnp.float32),
            pltpu.VMEM((PARTS, nd, 2 * tokens // LANES, LANES), jnp.float32),
            pltpu.VMEM((PARTS, tokens, features), jnp.bfloat16),
            pltpu.VMEM((nt, features, width), jnp.bfloat16),
            pltpu.VMEM((nt, features, width), jnp.bfloat16),
            pltpu.VMEM((nt, nd, 1, features), jnp.float32),
            dma((PARTS, nd)), dma((PARTS, nd)), dma((nt,)), dma((nt,)),
            dma((PARTS, nt, nd)), dma((PARTS, nt, nd)), dma((PARTS, nd)), dma((PARTS, nd)),
            dma((PARTS, nd)), dma((PARTS, nd)), dma((nt,)), dma((nt,)),
            dma((nt, nd)), dma((nt, nd)), dma((5,)),
        ],
        compiler_params=pltpu.CompilerParams(
            collective_id=0, has_side_effects=True, vmem_limit_bytes=63 * 1024 * 1024
        ),
        name="value_path_backward",
    )(hidden_in, norm_gain, value_weight, query, key, grad, positions)


def solution(mesh):
    sizes = tuple(mesh.shape[axis] for axis in ("section", "dp", "tensor"))

    def local(hidden_in, norm_gain, value_weight, query, key, grad, positions):
        weight_grad, gain_grad, previous = shards(
            sizes, hidden_in, norm_gain, value_weight, query, key, grad, positions.reshape(1, -1)
        )
        return (weight_grad, gain_grad, previous[None])

    return jax.shard_map(
        local,
        mesh=mesh,
        in_specs=(
            P("section", ("dp", "tensor"), None),
            P("section", None),
            P("section", "dp", "tensor"),
            P("section", "dp", "tensor"),
            P("section", "dp", "tensor"),
            P("section", "dp", "tensor"),
            P("section", "dp"),
        ),
        out_specs=(
            P("section", "dp", "tensor"),
            P("section", None),
            P("section", ("dp", "tensor"), None),
        ),
        check_vma=False,
    )
```
